768 devices in a mesh: blk: 24 (over z, x_hi), rep: 32 (over x_lo, y, core).
Axes of the slice: x: 4 (x_hi: 2, x_lo: 2; x = x_hi * 2 + x_lo), y: 8, z: 12, core: 2. Of those that a mesh axis runs over, the one named last changes fastest.
Arguments:
- feats: bfloat16 [32, 6144, 128], P('rep', 'blk'), may hold values from -6 to 6
- cotan: bfloat16 [32, 6144, 256], P('rep', 'blk'), may hold values from -6 to 6
- weight: bfloat16 [128, 256], replicated, may hold values from -0.5 to 0.5
- cycle_adj: bfloat16 [32, 6144, 6144], P('rep', 'blk'), as said below
- remote_adj: bfloat16 [32, 6144, 1024], P('rep', 'blk'), may hold values from -0.25 to 0.25
- send_ids: int32 [32, 24, 32, 32], P('rep', 'blk'), may hold values from 0 to 255
- send_count: int32 [32, 24, 32], P('rep', 'blk'), may hold values from 1 to 32, as said below
Outputs:
- output_rows: bfloat16 [32, 6144, 256], P('rep', 'blk')
- grad_feats: float32 [32, 6144, 128], P('rep', 'blk')
- grad_weight: float32 [128, 256], replicated
The draws below stay inside these ranges and needn't reach their ends.
Inputs may be any that keep to these rules, and one draw needn't show every extreme that they name: cycle_adj[r] is symmetric: entry (i, j) equals entry (j, i) exactly. `send_count`: every row block has 32 live slots toward at least one group.
All inputs are finite; a program needn't handle non-finite values.
Results may differ from the reference program's by a relative error of at most 0.017.
Values may be sent and summed in bfloat16 or wider, within the bound.
A program may use at most 32 MiB of HBM per device.

```python
import math
import jax
import jax.numpy as jnp
from jax import lax

FEAT = 128
HID = 256
ROWS = 256
SLOTS = 32
GROUP = 6144
NODES = 196608
N_BLK = 24
N_REP = 32


def draw_cycle_adj(key, part):
    key = jax.random.fold_in(key, 11)
    base = jax.random.normal(key, (N_REP, GROUP, GROUP), jnp.float32)
    sym_weights = (base + jnp.swapaxes(base, 1, 2)) * (0.7071 / math.sqrt(GROUP))
    return sym_weights.astype(jnp.bfloat16)


def draw_send_count(key, part):
    key = jax.random.fold_in(key, 23)
    base = jax.random.randint(key, (N_REP, N_BLK, N_REP), 1, SLOTS + 1)
    heavy = jax.random.randint(jax.random.fold_in(key, 1), (1, 1, N_REP), 1, 3)
    counts = jnp.minimum(base * heavy, SLOTS)
    source = lax_iota((N_REP, N_BLK, N_REP), 0)
    block = lax_iota((N_REP, N_BLK, N_REP), 1)
    target = lax_iota((N_REP, N_BLK, N_REP), 2)
    full_slot = target == (source * 5 + block * 3 + 1) % N_REP
    return jnp.where(full_slot, SLOTS, counts).astype(jnp.int32)


def lax_iota(shape, dimension):
    return jax.lax.broadcasted_iota(jnp.int32, shape, dimension)


def touch_ends(values, stream_key, low, high):
    place = [jax.random.randint(jax.random.fold_in(stream_key, axis), (), 0, length) for axis, length in enumerate(values.shape)]
    widest = values.shape.index(max(values.shape))
    neighbour = place[:widest] + [(place[widest] + 1) % values.shape[widest]] + place[widest + 1:]
    return values.at[tuple(place)].set(low).at[tuple(neighbour)].set(high)


def shard_levels(key, shape, cuts, least, largest):
    gain, own = 1.0, jax.random.fold_in(key, 6)
    for position, shards_of in cuts:
        steps = jnp.exp(jax.random.uniform(jax.random.fold_in(own, position), (shards_of,), jnp.float32, least / len(cuts), largest / len(cuts)))
        gain = gain * jnp.repeat(steps, shape[position] // shards_of).reshape([-1 if axis == position else 1 for axis in range(len(shape))])
    return gain


def bell_draw(own_key, extent, scale, limit, pieces=(), kind=jnp.bfloat16):
    level = shard_levels(own_key, extent, pieces, -0.22, 0.18) if pieces else 1.0
    entries = jax.random.normal(own_key, extent, jnp.float32) * scale * level
    return jnp.minimum(jnp.maximum(entries, -limit), limit).astype(kind)


def setup_inputs(seed: int = 0) -> dict:
    keys = jax.random.split(jax.random.key(seed), 8)
    feats = bell_draw(keys[0], (N_REP, GROUP, FEAT), 1.0, 6.0, ((0, 32), (1, 24)))
    cotan = bell_draw(keys[1], (N_REP, GROUP, HID), 1.0, 6.0, ((0, 32), (1, 24)))
    weight = bell_draw(keys[2], (FEAT, HID), FEAT ** -0.5, 0.5)
    cycle_adj = draw_cycle_adj(jax.random.fold_in(keys[7], 71), 0)
    remote_adj = bell_draw(keys[4], (N_REP, GROUP, N_REP * SLOTS), (N_REP * SLOTS // 2) ** -0.5, 0.25, ((0, 32), (1, 24)))
    send_ids = touch_ends(jax.random.randint(keys[5], (N_REP, N_BLK, N_REP, SLOTS), 0, ROWS), jax.random.fold_in(keys[5], 1), 0, ROWS - 1).astype(jnp.int32)
    send_count = draw_send_count(jax.random.fold_in(keys[7], 71), 0)
    return dict(feats=feats, cotan=cotan, weight=weight, cycle_adj=cycle_adj, remote_adj=remote_adj, send_ids=send_ids, send_count=send_count)


def gelu_tanh(values):
    return jax.nn.gelu(values, approximate=True)

def reference(feats, cotan, weight, cycle_adj, remote_adj, send_ids, send_count):
    cycle_agg = lax.map(lambda pair: jnp.dot(pair[0], pair[1], preferred_element_type=jnp.float32), (cycle_adj, feats))
    block_base = (jnp.arange(N_BLK, dtype=jnp.int32) * ROWS)[None, :, None, None]
    global_rows = (send_ids + block_base).astype(jnp.int32)
    group_index = jnp.arange(N_REP, dtype=jnp.int32)[:, None, None, None]
    picked = feats[group_index, global_rows]
    live_slots = jnp.arange(SLOTS, dtype=jnp.int32)[None, None, None, :] < send_count[..., None]
    sent = jnp.where(live_slots[..., None], picked, jnp.zeros_like(picked))
    arrived = jnp.transpose(sent, (2, 1, 0, 3, 4)).reshape(N_REP, N_BLK, N_REP * SLOTS, FEAT)
    far_adj = remote_adj.reshape(N_REP, N_BLK, ROWS, N_REP * SLOTS)
    far_agg = lax.map(lambda pair: jnp.einsum('bij,bjf->bif', pair[0].astype(jnp.float32), pair[1].astype(jnp.float32)), (far_adj, arrived))
    agg = (cycle_agg + far_agg.reshape(N_REP, GROUP, FEAT)).astype(jnp.bfloat16)
    flat_agg = agg.reshape(N_REP * GROUP, FEAT)
    pre_act = jnp.dot(flat_agg, weight, preferred_element_type=jnp.float32)
    activated, back_fn = jax.vjp(gelu_tanh, pre_act)
    output_rows = activated.astype(jnp.bfloat16).reshape(N_REP, GROUP, HID)
    dpre = back_fn(cotan.reshape(N_REP * GROUP, HID).astype(jnp.float32))[0].astype(jnp.bfloat16)
    grad_weight = lax.dot_general(flat_agg, dpre, (((0,), (0,)), ((), ())), preferred_element_type=jnp.float32) * (1.0 / math.sqrt(NODES))
    proj = lax.dot_general(dpre, weight, (((1,), (1,)), ((), ())), preferred_element_type=jnp.float32).astype(jnp.bfloat16)
    proj = proj.reshape(N_REP, GROUP, FEAT)
    cycle_back = lax.map(lambda pair: lax.dot_general(pair[0], pair[1], (((0,), (0,)), ((), ())), preferred_element_type=jnp.float32), (cycle_adj, proj))
    proj_blocks = proj.reshape(N_REP, N_BLK, ROWS, FEAT)
    far_terms = lax.map(lambda pair: jnp.einsum('bij,bif->bjf', pair[0].astype(jnp.float32), pair[1].astype(jnp.float32)).astype(jnp.bfloat16), (far_adj, proj_blocks))
    far_terms = far_terms.reshape(N_REP, N_BLK, N_REP, SLOTS, FEAT)
    returned = jnp.transpose(far_terms, (2, 1, 0, 3, 4)).astype(jnp.float32)
    masked = jnp.where(live_slots[..., None], returned, jnp.zeros_like(returned))
    group_full = jnp.broadcast_to(group_index, global_rows.shape)
    far_back = jnp.zeros((N_REP, GROUP, FEAT), jnp.float32).at[group_full, global_rows].add(masked)
    grad_feats = cycle_back + far_back
    return (output_rows, grad_feats, grad_weight)
```

```python
import functools
import math

import jax
import jax.numpy as jnp
from jax import lax
from jax.experimental import pallas as pl
from jax.experimental.pallas import tpu as pltpu
from jax.sharding import PartitionSpec as P

MESH = pl.DeviceIdType.MESH
F32 = jnp.float32
BF16 = jnp.bfloat16


def dot(a, b, dims=((1,), (0,))):
    return lax.dot_general(a, b, (dims, ((), ())), preferred_element_type=F32)


def layer_kernel(
    n_blk, n_rep,
    feats, cotan, weight, adj_hbm, far_hbm, ids, counts,
    out_rows, grad_feats, grad_weight,
    adj, far, near_x, near_p, total, pick, sent, arrived, back, returned, part, sum_rep, sum_blk, whole,
    load_sem, ring_send, ring_recv, pair_recv, swap_send, swap_recv, grad_send, grad_recv,
):
    blk = lax.axis_index("blk")
    rep = lax.axis_index("rep")
    rows, width = feats.shape[1], feats.shape[2]
    groups, slots = ids.shape[2], ids.shape[3]
    slot_total = groups * slots
    n_z = n_blk // 2
    reach = n_z // 2
    z = blk // 2
    x_hi = lax.rem(blk, 2)
    half = rows // 2
    piece = part.shape[1]

    barrier = pltpu.get_barrier_semaphore()

    def greet_rep(i, carry):
        pl.semaphore_signal(barrier, inc=1, device_id={"rep": lax.rem(rep + i, n_rep)}, device_id_type=MESH)
        return carry

    def greet_blk(i, carry):
        pl.semaphore_signal(barrier, inc=1, device_id={"blk": lax.rem(blk + i, n_blk)}, device_id_type=MESH)
        return carry

    lax.fori_loop(1, n_rep, greet_rep, 0)
    lax.fori_loop(1, n_blk, greet_blk, 0)

    load_adj = pltpu.make_async_copy(adj_hbm.at[0], adj, load_sem.at[0])
    load_far = pltpu.make_async_copy(far_hbm.at[0], far, load_sem.at[1])
    load_adj.start()
    load_far.start()

    def line(z_at, other):
        return lax.rem(z_at + n_z, n_z) * 2 + (1 - x_hi if other else x_hi)

    ups = (line(z + 1, 0), line(z - 1, 0))

    def hop(near, phase, way, other, d, idx):
        if isinstance(d, int) and d == reach:
            span = pl.ds(way * half, half)
        else:
            span = pl.ds(0, rows)
        return pltpu.make_async_remote_copy(
            src_ref=near.at[idx, span], dst_ref=near.at[idx, span],
            send_sem=ring_send.at[phase], recv_sem=ring_recv.at[phase, way, other, d - 1],
            device_id={"blk": ups[way]}, device_id_type=MESH,
        )

    def pair(near, phase, idx):
        return pltpu.make_async_remote_copy(
            src_ref=near.at[idx], dst_ref=near.at[idx],
            send_sem=ring_send.at[phase], recv_sem=pair_recv.at[phase],
            device_id={"blk": line(z, 1)}, device_id_type=MESH,
        )

    def add_block(near, idx):
        columns = pl.ds(pl.multiple_of(idx * rows, rows), rows)
        total[...] += dot(adj[:, columns], near[idx])

    def came(way, other, d):
        return line(z - d if way == 0 else z + d, other)

    def ring_open(near, phase):
        hop(near, phase, 0, 0, 1, blk).start()
        hop(near, phase, 1, 0, 1, blk).start()
        pair(near, phase, blk).start()

    def ring_pair(near, phase):
        idx = line(z, 1)
        pair(near, phase, idx).wait_recv()
        hop(near, phase, 0, 1, 1, idx).start()
        hop(near, phase, 1, 1, 1, idx).start()
        add_block(near, idx)

    def ring_step(near, phase, d, last):
        for other in (0, 1):
            for way in (0, 1):
                idx = came(way, other, d)
                hop(near, phase, way, other, d, idx).wait_recv()
                hop(near, phase, way, other, reach if last else d + 1, idx).start()
            for way in (0, 1):
                add_block(near, came(way, other, d))

    def ring_steps(near, phase, first, stop):
        def step(d, carry):
            ring_step(near, phase, d, False)
            return carry
        lax.fori_loop(first, stop, step, 0)

    def ring_close(near, phase):
        for other in (0, 1):
            idx = came(0, other, reach)
            for way in (0, 1):
                hop(near, phase, way, other, reach, idx).wait_recv()
            add_block(near, idx)

    def ring_drain(near, phase):
        whole_ring = near.at[pl.ds(0, n_blk - 1)]
        pltpu.make_async_copy(whole_ring, whole_ring, ring_send.at[phase]).wait()

    def to_reps(src, dst, send_sem, recv_sem):
        def send(i, carry):
            peer = lax.rem(rep + i, n_rep)
            pltpu.make_async_remote_copy(
                src_ref=src(peer), dst_ref=dst, send_sem=send_sem, recv_sem=recv_sem,
                device_id={"rep": peer}, device_id_type=MESH,
            ).start()
            return carry
        lax.fori_loop(1, n_rep, send, 0)

    def wait_all(ref, count, sem):
        span = ref.at[pl.ds(0, count)]
        pltpu.make_async_copy(span, span, sem).wait()

    spread = lax.broadcasted_iota(jnp.int32, (slots, slot_total), 1)
    within = spread - (spread // slots) * slots
    place = lax.broadcasted_iota(jnp.int32, (slots, slot_total), 0)
    per_slot = jnp.where(within == place, 1.0, 0.0).astype(BF16)
    spread_g = lax.broadcasted_iota(jnp.int32, (groups, slot_total), 1)
    own_group = (spread_g // slots) == lax.broadcasted_iota(jnp.int32, (groups, slot_total), 0)
    per_group = jnp.where(own_group, 1.0, 0.0).astype(BF16)
    ids_wide = dot(ids[0, 0].astype(F32).astype(BF16), per_slot)
    ids_row = jnp.sum(jnp.where(own_group, ids_wide, 0.0), axis=0, keepdims=True)
    counts_low = jnp.broadcast_to(counts[0].astype(F32), (8, groups)).astype(BF16)
    counts_row = dot(counts_low, per_group)[0:1]
    live = within[0:1].astype(F32) < counts_row
    ids_row = jnp.where(live, ids_row, -1.0).astype(jnp.int32)
    row_iota = lax.broadcasted_iota(jnp.int32, (rows, slot_total), 0)
    pick[...] = jnp.where(row_iota == ids_row, 1.0, 0.0).astype(BF16)
    own_feats = feats[0]
    near_x[blk] = own_feats
    sent[...] = dot(pick[...], own_feats, ((0,), (0,))).astype(BF16).reshape(groups, slots, width)

    pl.semaphore_wait(barrier, n_rep - 1 + n_blk - 1)

    ring_open(near_x, 0)
    to_reps(lambda peer: sent.at[peer], arrived.at[rep], swap_send.at[0], swap_recv.at[0])
    arrived[rep] = sent[rep]
    total[...] = jnp.zeros_like(total)
    load_adj.wait()
    add_block(near_x, blk)
    ring_pair(near_x, 0)
    ring_steps(near_x, 0, 1, reach - 1)
    ring_step(near_x, 0, reach - 1, True)
    load_far.wait()
    wait_all(arrived, n_rep - 1, swap_recv.at[0])
    total[...] += dot(far[...], arrived[...].reshape(slot_total, width))
    ring_close(near_x, 0)

    agg = total[...].astype(BF16)
    pre = dot(agg, weight[...])
    scale, cubic = 0.7978845608028654, 0.044715
    square = pre * pre
    bend = jnp.tanh(scale * pre * (1.0 + cubic * square))
    slope = 0.5 * (1.0 + bend) + 0.5 * pre * (1.0 - bend * bend) * (scale * (1.0 + 3.0 * cubic * square))
    dpre = (cotan[0].astype(F32) * slope).astype(BF16)
    proj = dot(dpre, weight[...], ((1,), (1,))).astype(BF16)
    near_p[blk] = proj
    ring_open(near_p, 1)
    share = dot(agg, dpre, ((0,), (0,)))
    per_half = n_rep // 2
    part[pl.ds(0, per_half)] = share[:, :width].reshape(per_half, piece, width)
    part[pl.ds(per_half, per_half)] = share[:, width:].reshape(per_half, piece, width)
    to_reps(lambda peer: part.at[peer], sum_rep.at[rep], grad_send.at[0], grad_recv.at[0])
    sum_rep[rep] = part[rep]
    back[...] = dot(far[...], proj, ((0,), (0,))).astype(BF16).reshape(groups, slots, width)
    to_reps(lambda peer: back.at[peer], returned.at[rep], swap_send.at[1], swap_recv.at[1])
    returned[rep] = back[rep]
    out_rows[0] = (0.5 * pre * (1.0 + bend)).astype(BF16)

    total[...] = jnp.zeros_like(total)
    add_block(near_p, blk)
    ring_pair(near_p, 1)
    first = min(3, reach - 1)
    ring_steps(near_p, 1, 1, first)

    wait_all(sum_rep, n_rep - 1, grad_recv.at[0])
    sum_blk[blk] = jnp.sum(sum_rep[...], axis=0)

    def send_blk(i, carry):
        pltpu.make_async_remote_copy(
            src_ref=sum_blk.at[blk], dst_ref=sum_blk.at[blk], send_sem=grad_send.at[1], recv_sem=grad_recv.at[1],
            device_id={"blk": lax.rem(blk + i, n_blk)}, device_id_type=MESH,
        ).start()
        return carry
    lax.fori_loop(1, n_blk, send_blk, 0)

    ring_steps(near_p, 1, first, reach - 1)
    wait_all(sum_blk, n_blk - 1, grad_recv.at[1])
    nodes = rows * n_blk * n_rep
    whole[rep] = jnp.sum(sum_blk[...], axis=0) * (1.0 / math.sqrt(nodes))
    to_reps(lambda peer: whole.at[rep], whole.at[rep], grad_send.at[2], grad_recv.at[2])
    ring_step(near_p, 1, reach - 1, True)
    wait_all(returned, n_rep - 1, swap_recv.at[1])
    total[...] += dot(pick[...], returned[...].reshape(slot_total, width))
    ring_close(near_p, 1)
    grad_feats[0] = total[...]
    wait_all(whole, n_rep - 1, grad_recv.at[2])
    flat = per_half * piece
    grad_weight[:, :width] = whole[pl.ds(0, per_half)].reshape(flat, width)
    grad_weight[:, width:] = whole[pl.ds(per_half, per_half)].reshape(flat, width)

    ring_drain(near_x, 0)
    ring_drain(near_p, 1)
    wait_all(sent, n_rep - 1, swap_send.at[0])
    wait_all(back, n_rep - 1, swap_send.at[1])
    wait_all(part, n_rep - 1, grad_send.at[0])
    wait_all(sum_blk, n_blk - 1, grad_send.at[1])
    wait_all(whole, n_rep - 1, grad_send.at[2])


def local(n_blk, n_rep, feats, cotan, weight, cycle_adj, remote_adj, send_ids, send_count):
    rows, width = feats.shape[1:]
    hidden = cotan.shape[2]
    groups, slots = send_ids.shape[2:]
    total = n_blk * rows
    reach = n_blk // 4
    piece = hidden // n_rep * (width // 128)
    vmem = pl.BlockSpec(memory_space=pltpu.VMEM)
    anywhere = pl.BlockSpec(memory_space=pl.ANY)
    dma = pltpu.SemaphoreType.DMA
    return pl.pallas_call(
        functools.partial(layer_kernel, n_blk, n_rep),
        out_shape=(
            jax.ShapeDtypeStruct((1, rows, hidden), BF16),
            jax.ShapeDtypeStruct((1, rows, width), F32),
            jax.ShapeDtypeStruct((width, hidden), F32),
        ),
        in_specs=[vmem, vmem, vmem, anywhere, anywhere, vmem, vmem],
        out_specs=(vmem, vmem, vmem),
        scratch_shapes=[
            pltpu.VMEM((rows, total), BF16),
            pltpu.VMEM((rows, groups * slots), BF16),
            pltpu.VMEM((n_blk, rows, width), BF16),
            pltpu.VMEM((n_blk, rows, width), BF16),
            pltpu.VMEM((rows, width), F32),
            pltpu.VMEM((rows, groups * slots), BF16),
            pltpu.VMEM((groups, slots, width), BF16),
            pltpu.VMEM((groups, slots, width), BF16),
            pltpu.VMEM((groups, slots, width), BF16),
            pltpu.VMEM((groups, slots, width), BF16),
            pltpu.VMEM((n_rep, piece, width), F32),
            pltpu.VMEM((n_rep, piece, width), F32),
            pltpu.VMEM((n_blk, piece, width), F32),
            pltpu.VMEM((n_rep, piece, width), F32),
            dma((2,)),
            dma((2,)),
            dma((2, 2, 2, reach)),
            dma((2,)),
            dma((2,)),
            dma((2,)),
            dma((3,)),
            dma((3,)),
        ],
        compiler_params=pltpu.CompilerParams(
            collective_id=0, has_side_effects=True, vmem_limit_bytes=40 * 1024 * 1024
        ),
    )(feats, cotan, weight, cycle_adj, remote_adj, send_ids, send_count)


def solution(mesh):
    n_blk, n_rep = mesh.shape["blk"], mesh.shape["rep"]
    return jax.shard_map(
        functools.partial(local, n_blk, n_rep),
        mesh=mesh,
        in_specs=(
            P("rep", "blk", None),
            P("rep", "blk", None),
            P(),
            P("rep", "blk", None),
            P("rep", "blk", None),
            P("rep", "blk", None, None),
            P("rep", "blk", None),
        ),
        out_specs=(P("rep", "blk", None), P("rep", "blk", None), P()),
        check_vma=False,
    )
```

```python
import functools
import math

import jax
import jax.numpy as jnp
from jax import lax
from jax.experimental import pallas as pl
from jax.experimental.pallas import tpu as pltpu
from jax.sharding import PartitionSpec as P

MESH = pl.DeviceIdType.MESH
F32 = jnp.float32
BF16 = jnp.bfloat16


def dot(a, b, dims=((1,), (0,))):
    return lax.dot_general(a, b, (dims, ((), ())), preferred_element_type=F32)

ROUTE = (
    (-1, 0, 1, 0, 16, 12),
    (-1, 2, 0, 0, 16, 4),
    (-1, -2, 0, 0, 16, 5),
    (-1, 1, 0, 0, 16, 13),
    (-1, -1, 0, 0, 16, 14),
    (1, 0, 1, 0, 16, 19),
    (2, 0, 1, 0, 16, 20),
    (1, 3, 0, 0, 16, 0),
    (2, -3, 0, 0, 16, 1),
    (3, 0, 1, 0, 16, 15),
    (1, 1, 0, 0, 16, 10),
    (2, -1, 0, 0, 16, 11),
    (4, 0, 1, 0, 16, 16),
    (5, 1, 0, 0, 16, 17),
    (6, -1, 0, 0, 16, 18),
    (7, 1, 0, 0, 8, 8),
    (8, -1, 0, 8, 16, 9),
    (7, 1, 1, 0, 8, 6),
    (7, 0, 1, 0, 16, 23),
    (10, 1, 0, 0, 16, 21),
    (11, -1, 0, 0, 16, 22),
    (8, -1, 1, 8, 16, 7),
    (13, 1, 0, 0, 16, 2),
    (8, 0, 1, 0, 16, 24),
    (14, -1, 0, 0, 16, 3),
)
GRAD_AT = (8, 18, 21)


def route_places():
    places = []
    for parent, dz, other, *_ in ROUTE:
        at = (0, 0) if parent < 0 else places[parent]
        places.append((at[0] - dz, at[1] ^ other))
    return places


def passed_on(parent):
    return sorted((k for k, entry in enumerate(ROUTE) if entry[0] == parent), key=lambda k: ROUTE[k][5])


def far_first(count):
    return sorted(range(count), key=lambda step: -min(step, count - step))


def layer_kernel(
    n_blk, n_rep,
    feats_hbm, cotan_hbm, weight_hbm, adj_hbm, far_hbm, ids_hbm, counts_hbm,
    out_rows, grad_feats, grad_weight,
    feats, cotan, weight, ids, counts,
    adj, far, near_x, near_p, total, pick, sent, arrived, back, returned, part, sum_rep, sum_blk, whole,
    load_sem, ring_send, ring_recv, swap_send, swap_recv, grad_send, grad_recv,
):
    blk = lax.axis_index("blk")
    rep = lax.axis_index("rep")
    rows, width = feats.shape
    groups, slots = ids.shape
    slot_total = groups * slots
    n_z = n_blk // 2
    n_y = n_rep // 4
    z = blk // 2
    x_hi = lax.rem(blk, 2)
    unit = rows // 16
    piece = part.shape[1]
    places = route_places()
    hops = sorted({(dz, other) for _, dz, other, *_ in ROUTE})

    def block_at(dz, other):
        return lax.rem(z + dz + 2 * n_z, n_z) * 2 + (1 - x_hi if other else x_hi)

    def rep_at(dy, low, core):
        x_low, y, own = rep // (2 * n_y), lax.rem(rep // 2, n_y), lax.rem(rep, 2)
        return lax.rem(x_low + low, 2) * (2 * n_y) + lax.rem(y + dy, n_y) * 2 + lax.rem(own + core, 2)

    barrier = pltpu.get_barrier_semaphore()

    for hop in hops:
        pl.semaphore_signal(barrier, inc=1, device_id={"blk": block_at(*hop)}, device_id_type=MESH)

    def greet_rep(i, carry):
        pl.semaphore_signal(barrier, inc=1, device_id={"rep": lax.rem(rep + i, n_rep)}, device_id_type=MESH)
        return carry

    lax.fori_loop(1, n_rep, greet_rep, 0)

    loads = [
        pltpu.make_async_copy(src, dst, load_sem.at[i])
        for i, (src, dst) in enumerate((
            (feats_hbm.at[0], feats), (ids_hbm.at[0, 0], ids), (counts_hbm.at[0], counts),
            (adj_hbm.at[0], adj), (far_hbm.at[0], far), (cotan_hbm.at[0], cotan), (weight_hbm, weight),
        ))
    ]
    for load in loads:
        load.start()

    def copy_on(near, phase, k):
        parent, dz, other, low, high, _ = ROUTE[k]
        at = block_at(*(places[parent] if parent >= 0 else (0, 0)))
        span = near.at[at, pl.ds(low * unit, (high - low) * unit)]
        return pltpu.make_async_remote_copy(
            src_ref=span, dst_ref=span, send_sem=ring_send.at[phase], recv_sem=ring_recv.at[phase, k],
            device_id={"blk": block_at(dz, other)}, device_id_type=MESH,
        )

    def wait_copy(near, phase, k):
        low, high = ROUTE[k][3:5]
        span = near.at[block_at(*places[k]), pl.ds(low * unit, (high - low) * unit)]
        pltpu.make_async_copy(span, span, ring_recv.at[phase, k]).wait()

    def add_block(near, idx):
        columns = pl.ds(pl.multiple_of(idx * rows, rows), rows)
        total[...] += dot(adj[:, columns], near[idx])

    def ring_open(near, phase):
        for k in passed_on(-1):
            copy_on(near, phase, k).start()

    def ring_run(near, phase, between):
        seen = {}
        for k in range(len(ROUTE)):
            wait_copy(near, phase, k)
            for child in passed_on(k):
                copy_on(near, phase, child).start()
            place = (places[k][0] % n_z, places[k][1])
            seen[place] = seen.get(place, 0) + ROUTE[k][4] - ROUTE[k][3]
            if seen[place] == 16:
                add_block(near, block_at(*place))
            for task in between.get(k, ()):
                task()

    def ring_drain(near, phase):
        whole_ring = near.at[pl.ds(0, n_blk - 1)]
        pltpu.make_async_copy(whole_ring, whole_ring, ring_send.at[phase]).wait()

    def to_reps(src, dst, send_sem, recv_sem, steps):
        for dy in steps:
            def send(i, carry, dy=dy):
                peer = rep_at(dy, i // 2, lax.rem(i, 2))
                pltpu.make_async_remote_copy(
                    src_ref=src(peer), dst_ref=dst, send_sem=send_sem, recv_sem=recv_sem,
                    device_id={"rep": peer}, device_id_type=MESH,
                ).start()
                return carry
            lax.fori_loop(0 if dy else 1, 4, send, 0)

    def wait_all(ref, count, sem):
        span = ref.at[pl.ds(0, count)]
        pltpu.make_async_copy(span, span, sem).wait()

    far_y = far_first(n_y)
    loads[0].wait()
    own_feats = feats[...]
    near_x[blk] = own_feats
    pl.semaphore_wait(barrier, n_rep - 1 + len(hops))
    ring_open(near_x, 0)

    spread = lax.broadcasted_iota(jnp.int32, (slots, slot_total), 1)
    within = spread - (spread // slots) * slots
    place = lax.broadcasted_iota(jnp.int32, (slots, slot_total), 0)
    per_slot = jnp.where(within == place, 1.0, 0.0).astype(BF16)
    spread_g = lax.broadcasted_iota(jnp.int32, (groups, slot_total), 1)
    own_group = (spread_g // slots) == lax.broadcasted_iota(jnp.int32, (groups, slot_total), 0)
    per_group = jnp.where(own_group, 1.0, 0.0).astype(BF16)
    loads[1].wait()
    ids_wide = dot(ids[...].astype(F32).astype(BF16), per_slot)
    ids_row = jnp.sum(jnp.where(own_group, ids_wide, 0.0), axis=0, keepdims=True)
    loads[2].wait()
    counts_low = jnp.broadcast_to(counts[...].astype(F32), (8, groups)).astype(BF16)
    counts_row = dot(counts_low, per_group)[0:1]
    live = within[0:1].astype(F32) < counts_row
    ids_row = jnp.where(live, ids_row, -1.0).astype(jnp.int32)
    row_iota = lax.broadcasted_iota(jnp.int32, (rows, slot_total), 0)
    pick[...] = jnp.where(row_iota == ids_row, 1.0, 0.0).astype(BF16)
    sent[...] = dot(pick[...], own_feats, ((0,), (0,))).astype(BF16).reshape(groups, slots, width)
    to_reps(lambda peer: sent.at[peer], arrived.at[rep], swap_send.at[0], swap_recv.at[0], far_y)
    arrived[rep] = sent[rep]

    total[...] = jnp.zeros_like(total)
    loads[3].wait()
    add_block(near_x, blk)

    def add_far():
        loads[4].wait()
        wait_all(arrived, n_rep - 1, swap_recv.at[0])
        total[...] += dot(far[...], arrived[...].reshape(slot_total, width))

    ring_run(near_x, 0, {len(ROUTE) - 5: (add_far,)})

    agg = total[...].astype(BF16)
    loads[5].wait()
    loads[6].wait()
    pre = dot(agg, weight[...])
    scale, cubic = 0.7978845608028654, 0.044715
    square = pre * pre
    bend = jnp.tanh(scale * pre * (1.0 + cubic * square))
    slope = 0.5 * (1.0 + bend) + 0.5 * pre * (1.0 - bend * bend) * (scale * (1.0 + 3.0 * cubic * square))
    dpre = (cotan[...].astype(F32) * slope).astype(BF16)
    proj = dot(dpre, weight[...], ((1,), (1,))).astype(BF16)
    near_p[blk] = proj
    ring_open(near_p, 1)
    share = dot(agg, dpre, ((0,), (0,)))
    per_half = n_rep // 2
    part[pl.ds(0, per_half)] = share[:, :width].reshape(per_half, piece, width)
    part[pl.ds(per_half, per_half)] = share[:, width:].reshape(per_half, piece, width)
    to_reps(lambda peer: part.at[peer], sum_rep.at[rep], grad_send.at[0], grad_recv.at[0], far_y)
    sum_rep[rep] = part[rep]
    out_rows[0] = (0.5 * pre * (1.0 + bend)).astype(BF16)
    back[...] = dot(far[...], proj, ((0,), (0,))).astype(BF16).reshape(groups, slots, width)
    returned[rep] = back[rep]
    total[...] = jnp.zeros_like(total)
    add_block(near_p, blk)

    def swap_back(steps):
        return lambda: to_reps(lambda peer: back.at[peer], returned.at[rep], swap_send.at[1], swap_recv.at[1], steps)

    def grad_blk():
        wait_all(sum_rep, n_rep - 1, grad_recv.at[0])
        sum_blk[blk] = jnp.sum(sum_rep[...], axis=0)
        for dz in far_first(n_z):
            for other in (1, 0):
                if dz or other:
                    pltpu.make_async_remote_copy(
                        src_ref=sum_blk.at[blk], dst_ref=sum_blk.at[blk],
                        send_sem=grad_send.at[1], recv_sem=grad_recv.at[1],
                        device_id={"blk": block_at(dz, other)}, device_id_type=MESH,
                    ).start()

    def grad_whole():
        wait_all(sum_blk, n_blk - 1, grad_recv.at[1])
        nodes = rows * n_blk * n_rep
        whole[rep] = jnp.sum(sum_blk[...], axis=0) * (1.0 / math.sqrt(nodes))
        to_reps(lambda peer: whole.at[rep], whole.at[rep], grad_send.at[2], grad_recv.at[2], far_y)

    def add_returned():
        wait_all(returned, n_rep - 1, swap_recv.at[1])
        total[...] += dot(pick[...], returned[...].reshape(slot_total, width))

    quarter = max(1, n_y // 4)
    tasks = {0: [swap_back(far_y[:quarter])], 2: [swap_back(far_y[quarter:2 * quarter])],
             4: [swap_back(far_y[2 * quarter:3 * quarter])], 5: [swap_back(far_y[3 * quarter:])]}
    for at, task in ((GRAD_AT[0], grad_blk), (GRAD_AT[1], grad_whole), (GRAD_AT[2], add_returned)):
        tasks.setdefault(at, []).append(task)
    ring_run(near_p, 1, tasks)

    grad_feats[0] = total[...]
    wait_all(whole, n_rep - 1, grad_recv.at[2])
    flat = per_half * piece
    grad_weight[:, :width] = whole[pl.ds(0, per_half)].reshape(flat, width)
    grad_weight[:, width:] = whole[pl.ds(per_half, per_half)].reshape(flat, width)

    ring_drain(near_x, 0)
    ring_drain(near_p, 1)
    wait_all(sent, n_rep - 1, swap_send.at[0])
    wait_all(back, n_rep - 1, swap_send.at[1])
    wait_all(part, n_rep - 1, grad_send.at[0])
    wait_all(sum_blk, n_blk - 1, grad_send.at[1])
    wait_all(whole, n_rep - 1, grad_send.at[2])


def hand_out(rows_in, feats_in, weight_in, rows_out, feats_out, weight_out, rows, feats, weight, sem):
    stages = ((rows_in, rows, rows_out), (feats_in, feats, feats_out), (weight_in, weight, weight_out))
    fetches = [pltpu.make_async_copy(src, held, sem.at[0, i]) for i, (src, held, _) in enumerate(stages)]
    stores = [pltpu.make_async_copy(held, dst, sem.at[1, i]) for i, (_, held, dst) in enumerate(stages)]
    for fetch in fetches:
        fetch.start()
    for fetch, store in zip(fetches, stores):
        fetch.wait()
        store.start()
    for store in stores:
        store.wait()


def local(n_blk, n_rep, feats, cotan, weight, cycle_adj, remote_adj, send_ids, send_count):
    rows, width = feats.shape[1:]
    hidden = cotan.shape[2]
    groups, slots = send_ids.shape[2:]
    total = n_blk * rows
    piece = hidden // n_rep * (width // 128)
    vmem = pl.BlockSpec(memory_space=pltpu.VMEM)
    anywhere = pl.BlockSpec(memory_space=pl.ANY)
    dma = pltpu.SemaphoreType.DMA
    results = pl.pallas_call(
        functools.partial(layer_kernel, n_blk, n_rep),
        out_shape=(
            jax.ShapeDtypeStruct((1, rows, hidden), BF16),
            jax.ShapeDtypeStruct((1, rows, width), F32),
            jax.ShapeDtypeStruct((width, hidden), F32),
        ),
        in_specs=[anywhere] * 7,
        out_specs=(vmem, vmem, vmem),
        scratch_shapes=[
            pltpu.VMEM((rows, width), BF16),
            pltpu.VMEM((rows, hidden), BF16),
            pltpu.VMEM((width, hidden), BF16),
            pltpu.VMEM((groups, slots), jnp.int32),
            pltpu.VMEM((1, groups), jnp.int32),
            pltpu.VMEM((rows, total), BF16),
            pltpu.VMEM((rows, groups * slots), BF16),
            pltpu.VMEM((n_blk, rows, width), BF16),
            pltpu.VMEM((n_blk, rows, width), BF16),
            pltpu.VMEM((rows, width), F32),
            pltpu.VMEM((rows, groups * slots), BF16),
            pltpu.VMEM((groups, slots, width), BF16),
            pltpu.VMEM((groups, slots, width), BF16),
            pltpu.VMEM((groups, slots, width), BF16),
            pltpu.VMEM((groups, slots, width), BF16),
            pltpu.VMEM((n_rep, piece, width), F32),
            pltpu.VMEM((n_rep, piece, width), F32),
            pltpu.VMEM((n_blk, piece, width), F32),
            pltpu.VMEM((n_rep, piece, width), F32),
            dma((7,)),
            dma((2,)),
            dma((2, len(ROUTE))),
            dma((2,)),
            dma((2,)),
            dma((3,)),
            dma((3,)),
        ],
        compiler_params=pltpu.CompilerParams(
            collective_id=0, has_side_effects=True, vmem_limit_bytes=60 * 1024 * 1024
        ),
    )(feats, cotan, weight, cycle_adj, remote_adj, send_ids, send_count)
    return pl.pallas_call(
        hand_out,
        out_shape=tuple(jax.ShapeDtypeStruct(value.shape, value.dtype) for value in results),
        in_specs=[anywhere] * 3,
        out_specs=(anywhere,) * 3,
        scratch_shapes=[pltpu.VMEM(value.shape, value.dtype) for value in results] + [dma((2, 3))],
        compiler_params=pltpu.CompilerParams(vmem_limit_bytes=60 * 1024 * 1024),
    )(*results)


def solution(mesh):
    n_blk, n_rep = mesh.shape["blk"], mesh.shape["rep"]
    return jax.shard_map(
        functools.partial(local, n_blk, n_rep),
        mesh=mesh,
        in_specs=(
            P("rep", "blk", None),
            P("rep", "blk", None),
            P(),
            P("rep", "blk", None),
            P("rep", "blk", None),
            P("rep", "blk", None, None),
            P("rep", "blk", None),
        ),
        out_specs=(P("rep", "blk", None), P("rep", "blk", None), P()),
        check_vma=False,
    )
```

```python
import functools
import math

import jax
import jax.numpy as jnp
from jax import lax
from jax.experimental import pallas as pl
from jax.experimental.pallas import tpu as pltpu
from jax.sharding import PartitionSpec as P

MESH = pl.DeviceIdType.MESH
F32 = jnp.float32
BF16 = jnp.bfloat16


def dot(a, b, dims=((1,), (0,))):
    return lax.dot_general(a, b, (dims, ((), ())), preferred_element_type=F32)

ROUTE = (
    (-1, 1, 0, 0, 8, 4),
    (-1, -1, 0, 0, 8, 5),
    (-1, 0, 1, 8, 16, 30),
    (-1, 0, 1, 0, 8, 35),
    (-1, 2, 0, 8, 16, 40),
    (-1, -2, 0, 8, 16, 41),
    (-1, 1, 0, 8, 16, 48),
    (-1, -1, 0, 8, 16, 49),
    (0, 0, 1, 0, 8, 22),
    (0, 2, 0, 0, 8, 10),
    (0, 1, 0, 0, 8, 20),
    (1, -2, 0, 0, 8, 11),
    (1, 0, 1, 0, 8, 23),
    (1, -1, 0, 0, 8, 21),
    (4, 1, 0, 8, 16, 18),
    (4, 0, 1, 8, 16, 2),
    (5, -1, 0, 8, 16, 19),
    (5, 0, 1, 8, 16, 3),
    (6, 0, 1, 8, 16, 8),
    (9, 1, 0, 0, 8, 14),
    (7, 0, 1, 8, 16, 9),
    (11, -1, 0, 0, 8, 15),
    (4, 4, 0, 8, 12, 36),
    (9, 0, 1, 0, 8, 31),
    (5, -4, 0, 12, 16, 37),
    (14, 1, 0, 8, 16, 33),
    (10, 0, 1, 0, 8, 16),
    (9, 3, 0, 0, 4, 42),
    (16, -1, 0, 8, 16, 34),
    (11, 0, 1, 0, 8, 32),
    (11, -3, 0, 4, 8, 43),
    (13, 0, 1, 0, 8, 17),
    (15, 2, 0, 8, 16, 26),
    (19, 1, 0, 0, 8, 0),
    (14, 0, 1, 8, 16, 24),
    (17, -2, 0, 8, 16, 27),
    (21, -1, 0, 0, 8, 1),
    (16, 0, 1, 8, 16, 25),
    (23, 1, 0, 0, 8, 12),
    (28, -1, 0, 8, 16, 39),
    (25, 1, 0, 8, 16, 38),
    (19, 1, 1, 0, 8, 6),
    (22, 0, 1, 8, 12, 44),
    (29, -1, 0, 0, 8, 13),
    (32, 1, 0, 8, 16, 28),
    (21, -1, 1, 0, 8, 7),
    (24, 0, 1, 12, 16, 45),
    (27, 0, 1, 0, 4, 46),
    (35, -1, 0, 8, 16, 29),
    (30, 0, 1, 4, 8, 47),
)
GRAD_AT = (10, 26, 46)
BACK_AT = (11, 13, 15, 17)


def route_places():
    places = []
    for parent, dz, other, *_ in ROUTE:
        at = (0, 0) if parent < 0 else places[parent]
        places.append((at[0] - dz, at[1] ^ other))
    return places


def passed_on(parent):
    return sorted((k for k, entry in enumerate(ROUTE) if entry[0] == parent), key=lambda k: ROUTE[k][5])


def far_first(count):
    return sorted(range(count), key=lambda step: -min(step, count - step))


def layer_kernel(
    n_blk, n_rep,
    feats_hbm, cotan_hbm, weight_hbm, adj_hbm, far_hbm, ids_hbm, counts_hbm,
    out_rows, grad_feats, grad_weight,
    feats, cotan, weight, ids, counts,
    adj, far, near_x, near_p, total, pick, sent, arrived, back, returned, part, sum_rep, sum_blk, whole,
    load_sem, ring_send, ring_recv, swap_send, swap_recv, grad_send, grad_recv,
):
    blk = lax.axis_index("blk")
    rep = lax.axis_index("rep")
    rows, width = feats.shape
    groups, slots = ids.shape
    slot_total = groups * slots
    n_z = n_blk // 2
    n_y = n_rep // 4
    z = blk // 2
    x_hi = lax.rem(blk, 2)
    unit = rows // 16
    piece = part.shape[1]
    places = route_places()
    hops = sorted({(dz, other) for _, dz, other, *_ in ROUTE})

    def block_at(dz, other):
        return lax.rem(z + dz + 2 * n_z, n_z) * 2 + (1 - x_hi if other else x_hi)

    x_low, y, core = rep // (2 * n_y), lax.rem(rep // 2, n_y), lax.rem(rep, 2)
    x_parts = (x_low * (2 * n_y), (1 - x_low) * (2 * n_y))
    y_parts = [lax.rem(y + dy, n_y) * 2 for dy in range(n_y)]
    core_parts = (core, 1 - core)
    steps = [(dy, dx, dc) for dy in range(n_y) for dx in (0, 1) for dc in (0, 1) if dy or dx or dc]
    steps.sort(key=lambda step: -min(step[0], n_y - step[0]) - step[1])
    peers = [x_parts[dx] + y_parts[dy] + core_parts[dc] for dy, dx, dc in steps]
    fourth = n_rep // 4
    fourths = [peers[i:i + fourth] for i in range(0, n_rep - 1, fourth)]

    barrier = pltpu.get_barrier_semaphore()

    for hop in hops:
        pl.semaphore_signal(barrier, inc=1, device_id={"blk": block_at(*hop)}, device_id_type=MESH)

    for peer in peers:
        pl.semaphore_signal(barrier, inc=1, device_id={"rep": peer}, device_id_type=MESH)

    loads = [
        pltpu.make_async_copy(src, dst, load_sem.at[i])
        for i, (src, dst) in enumerate((
            (feats_hbm.at[0], feats), (ids_hbm.at[0, 0], ids), (counts_hbm.at[0], counts),
            (adj_hbm.at[0], adj), (far_hbm.at[0], far), (cotan_hbm.at[0], cotan), (weight_hbm, weight),
        ))
    ]
    for load in loads:
        load.start()

    def copy_on(near, phase, k):
        parent, dz, other, low, high, _ = ROUTE[k]
        at = block_at(*(places[parent] if parent >= 0 else (0, 0)))
        span = near.at[at, pl.ds(low * unit, (high - low) * unit)]
        return pltpu.make_async_remote_copy(
            src_ref=span, dst_ref=span, send_sem=ring_send.at[phase], recv_sem=ring_recv.at[phase, k],
            device_id={"blk": block_at(dz, other)}, device_id_type=MESH,
        )

    def wait_copy(near, phase, k):
        low, high = ROUTE[k][3:5]
        span = near.at[block_at(*places[k]), pl.ds(low * unit, (high - low) * unit)]
        pltpu.make_async_copy(span, span, ring_recv.at[phase, k]).wait()

    def add_pair(near, dz):
        first = lax.rem(z + dz + n_z, n_z) * 2
        columns = pl.ds(pl.multiple_of(first * rows, 2 * rows), 2 * rows)
        total[...] += dot(adj[:, columns], near[pl.ds(first, 2)].reshape(2 * rows, width))

    def ring_open(near, phase):
        for k in passed_on(-1):
            copy_on(near, phase, k).start()

    def ring_run(near, phase, between):
        seen = {0: 16}
        for task in between.get(-1, ()):
            task()
        for k in range(len(ROUTE)):
            wait_copy(near, phase, k)
            for child in passed_on(k):
                copy_on(near, phase, child).start()
            place = places[k][0] % n_z
            seen[place] = seen.get(place, 0) + ROUTE[k][4] - ROUTE[k][3]
            if seen[place] == 32:
                add_pair(near, place)
            for task in between.get(k, ()):
                task()

    def ring_drain(near, phase):
        whole_ring = near.at[pl.ds(0, n_blk - 1)]
        pltpu.make_async_copy(whole_ring, whole_ring, ring_send.at[phase]).wait()

    def to_reps(src, dst, send_sem, recv_sem, chosen):
        for peer in chosen:
            pltpu.make_async_remote_copy(
                src_ref=src(peer), dst_ref=dst, send_sem=send_sem, recv_sem=recv_sem,
                device_id={"rep": peer}, device_id_type=MESH,
            ).start()

    def wait_all(ref, count, sem):
        span = ref.at[pl.ds(0, count)]
        pltpu.make_async_copy(span, span, sem).wait()

    loads[0].wait()
    own_feats = feats[...]
    near_x[blk] = own_feats
    pl.semaphore_wait(barrier, n_rep - 1 + len(hops))
    ring_open(near_x, 0)

    def make_pick():
        spread = lax.broadcasted_iota(jnp.int32, (slots, slot_total), 1)
        within = spread - (spread // slots) * slots
        place = lax.broadcasted_iota(jnp.int32, (slots, slot_total), 0)
        per_slot = jnp.where(within == place, 1.0, 0.0).astype(BF16)
        spread_g = lax.broadcasted_iota(jnp.int32, (groups, slot_total), 1)
        own_group = (spread_g // slots) == lax.broadcasted_iota(jnp.int32, (groups, slot_total), 0)
        per_group = jnp.where(own_group, 1.0, 0.0).astype(BF16)
        loads[1].wait()
        ids_wide = dot(ids[...].astype(F32).astype(BF16), per_slot)
        ids_row = jnp.sum(jnp.where(own_group, ids_wide, 0.0), axis=0, keepdims=True)
        loads[2].wait()
        counts_low = jnp.broadcast_to(counts[...].astype(F32), (8, groups)).astype(BF16)
        counts_row = dot(counts_low, per_group)[0:1]
        live = within[0:1].astype(F32) < counts_row
        ids_row = jnp.where(live, ids_row, -1.0).astype(jnp.int32)
        row_iota = lax.broadcasted_iota(jnp.int32, (rows, slot_total), 0)
        pick[...] = jnp.where(row_iota == ids_row, 1.0, 0.0).astype(BF16)

    def gather_slots():
        sent[...] = dot(pick[...], feats[...], ((0,), (0,))).astype(BF16).reshape(groups, slots, width)
        arrived[rep] = sent[rep]

    def swap_out(chosen):
        return lambda: to_reps(lambda peer: sent.at[peer], arrived.at[rep], swap_send.at[0], swap_recv.at[0], chosen)

    def ready_adj():
        total[...] = jnp.zeros_like(total)
        loads[3].wait()

    def add_far():
        loads[4].wait()
        wait_all(arrived, n_rep - 1, swap_recv.at[0])
        total[...] += dot(far[...], arrived[...].reshape(slot_total, width))

    ring_run(near_x, 0, {-1: [make_pick, gather_slots, swap_out(peers), ready_adj], len(ROUTE) - 8: [add_far]})

    agg = total[...].astype(BF16)
    loads[5].wait()
    loads[6].wait()
    pre = dot(agg, weight[...])
    scale, cubic = 0.7978845608028654, 0.044715
    square = pre * pre
    bend = jnp.tanh(scale * pre * (1.0 + cubic * square))
    slope = 0.5 * (1.0 + bend) + 0.5 * pre * (1.0 - bend * bend) * (scale * (1.0 + 3.0 * cubic * square))
    dpre = (cotan[...].astype(F32) * slope).astype(BF16)
    proj = dot(dpre, weight[...], ((1,), (1,))).astype(BF16)
    near_p[blk] = proj
    ring_open(near_p, 1)
    share = dot(agg, dpre, ((0,), (0,)))
    per_half = n_rep // 2
    part[pl.ds(0, per_half)] = share[:, :width].reshape(per_half, piece, width)
    part[pl.ds(per_half, per_half)] = share[:, width:].reshape(per_half, piece, width)
    to_reps(lambda peer: part.at[peer], sum_rep.at[rep], grad_send.at[0], grad_recv.at[0], peers)
    sum_rep[rep] = part[rep]
    total[...] = jnp.zeros_like(total)
    out_rows[0] = (0.5 * pre * (1.0 + bend)).astype(BF16)

    def make_back():
        back[...] = dot(far[...], near_p[blk], ((0,), (0,))).astype(BF16).reshape(groups, slots, width)
        returned[rep] = back[rep]

    def swap_back(chosen):
        return lambda: to_reps(lambda peer: back.at[peer], returned.at[rep], swap_send.at[1], swap_recv.at[1], chosen)

    def grad_blk():
        wait_all(sum_rep, n_rep - 1, grad_recv.at[0])
        sum_blk[blk] = jnp.sum(sum_rep[...], axis=0)
        for dz in far_first(n_z):
            for other in (1, 0):
                if dz or other:
                    pltpu.make_async_remote_copy(
                        src_ref=sum_blk.at[blk], dst_ref=sum_blk.at[blk],
                        send_sem=grad_send.at[1], recv_sem=grad_recv.at[1],
                        device_id={"blk": block_at(dz, other)}, device_id_type=MESH,
                    ).start()

    def grad_whole():
        wait_all(sum_blk, n_blk - 1, grad_recv.at[1])
        nodes = rows * n_blk * n_rep
        whole[rep] = jnp.sum(sum_blk[...], axis=0) * (1.0 / math.sqrt(nodes))
        to_reps(lambda peer: whole.at[rep], whole.at[rep], grad_send.at[2], grad_recv.at[2], peers)

    def add_returned():
        wait_all(returned, n_rep - 1, swap_recv.at[1])
        total[...] += dot(pick[...], returned[...].reshape(slot_total, width))

    tasks = {8: [make_back]}
    for at, chosen in zip(BACK_AT, fourths):
        tasks.setdefault(at, []).append(swap_back(chosen))
    for at, task in ((GRAD_AT[0], grad_blk), (GRAD_AT[1], grad_whole), (GRAD_AT[2], add_returned)):
        tasks.setdefault(at, []).append(task)
    ring_run(near_p, 1, tasks)

    grad_feats[0] = total[...]
    wait_all(whole, n_rep - 1, grad_recv.at[2])
    flat = per_half * piece
    grad_weight[:, :width] = whole[pl.ds(0, per_half)].reshape(flat, width)
    grad_weight[:, width:] = whole[pl.ds(per_half, per_half)].reshape(flat, width)

    ring_drain(near_x, 0)
    ring_drain(near_p, 1)
    wait_all(sent, n_rep - 1, swap_send.at[0])
    wait_all(back, n_rep - 1, swap_send.at[1])
    wait_all(part, n_rep - 1, grad_send.at[0])
    wait_all(sum_blk, n_blk - 1, grad_send.at[1])
    wait_all(whole, n_rep - 1, grad_send.at[2])


def hand_out(rows_in, feats_in, weight_in, rows_out, feats_out, weight_out, rows, feats, weight, sem):
    stages = ((rows_in, rows, rows_out), (feats_in, feats, feats_out), (weight_in, weight, weight_out))
    fetches = [pltpu.make_async_copy(src, held, sem.at[0, i]) for i, (src, held, _) in enumerate(stages)]
    stores = [pltpu.make_async_copy(held, dst, sem.at[1, i]) for i, (_, held, dst) in enumerate(stages)]
    for fetch in fetches:
        fetch.start()
    for fetch, store in zip(fetches, stores):
        fetch.wait()
        store.start()
    for store in stores:
        store.wait()


def local(n_blk, n_rep, feats, cotan, weight, cycle_adj, remote_adj, send_ids, send_count):
    rows, width = feats.shape[1:]
    hidden = cotan.shape[2]
    groups, slots = send_ids.shape[2:]
    total = n_blk * rows
    piece = hidden // n_rep * (width // 128)
    vmem = pl.BlockSpec(memory_space=pltpu.VMEM)
    anywhere = pl.BlockSpec(memory_space=pl.ANY)
    dma = pltpu.SemaphoreType.DMA
    results = pl.pallas_call(
        functools.partial(layer_kernel, n_blk, n_rep),
        out_shape=(
            jax.ShapeDtypeStruct((1, rows, hidden), BF16),
            jax.ShapeDtypeStruct((1, rows, width), F32),
            jax.ShapeDtypeStruct((width, hidden), F32),
        ),
        in_specs=[anywhere] * 7,
        out_specs=(vmem, vmem, vmem),
        scratch_shapes=[
            pltpu.VMEM((rows, width), BF16),
            pltpu.VMEM((rows, hidden), BF16),
            pltpu.VMEM((width, hidden), BF16),
            pltpu.VMEM((groups, slots), jnp.int32),
            pltpu.VMEM((1, groups), jnp.int32),
            pltpu.VMEM((rows, total), BF16),
            pltpu.VMEM((rows, groups * slots), BF16),
            pltpu.VMEM((n_blk, rows, width), BF16),
            pltpu.VMEM((n_blk, rows, width), BF16),
            pltpu.VMEM((rows, width), F32),
            pltpu.VMEM((rows, groups * slots), BF16),
            pltpu.VMEM((groups, slots, width), BF16),
            pltpu.VMEM((groups, slots, width), BF16),
            pltpu.VMEM((groups, slots, width), BF16),
            pltpu.VMEM((groups, slots, width), BF16),
            pltpu.VMEM((n_rep, piece, width), F32),
            pltpu.VMEM((n_rep, piece, width), F32),
            pltpu.VMEM((n_blk, piece, width), F32),
            pltpu.VMEM((n_rep, piece, width), F32),
            dma((7,)),
            dma((2,)),
            dma((2, len(ROUTE))),
            dma((2,)),
            dma((2,)),
            dma((3,)),
            dma((3,)),
        ],
        compiler_params=pltpu.CompilerParams(
            collective_id=0, has_side_effects=True, vmem_limit_bytes=60 * 1024 * 1024
        ),
    )(feats, cotan, weight, cycle_adj, remote_adj, send_ids, send_count)
    return pl.pallas_call(
        hand_out,
        out_shape=tuple(jax.ShapeDtypeStruct(value.shape, value.dtype) for value in results),
        in_specs=[anywhere] * 3,
        out_specs=(anywhere,) * 3,
        scratch_shapes=[pltpu.VMEM(value.shape, value.dtype) for value in results] + [dma((2, 3))],
        compiler_params=pltpu.CompilerParams(vmem_limit_bytes=60 * 1024 * 1024),
    )(*results)


def solution(mesh):
    n_blk, n_rep = mesh.shape["blk"], mesh.shape["rep"]
    return jax.shard_map(
        functools.partial(local, n_blk, n_rep),
        mesh=mesh,
        in_specs=(
            P("rep", "blk", None),
            P("rep", "blk", None),
            P(),
            P("rep", "blk", None),
            P("rep", "blk", None),
            P("rep", "blk", None, None),
            P("rep", "blk", None),
        ),
        out_specs=(P("rep", "blk", None), P("rep", "blk", None), P()),
        check_vma=False,
    )
```

```python
import functools
import math

import jax
import jax.numpy as jnp
from jax import lax
from jax.experimental import pallas as pl
from jax.experimental.pallas import tpu as pltpu
from jax.sharding import PartitionSpec as P

MESH = pl.DeviceIdType.MESH
F32 = jnp.float32
BF16 = jnp.bfloat16


def dot(a, b, dims=((1,), (0,))):
    return lax.dot_general(a, b, (dims, ((), ())), preferred_element_type=F32)

ROUTE = (
    (-1, 1, 0, 0, 8, 4),
    (-1, -1, 0, 0, 8, 5),
    (-1, 0, 1, 8, 16, 30),
    (-1, 0, 1, 0, 8, 35),
    (-1, 2, 0, 8, 16, 40),
    (-1, -2, 0, 8, 16, 41),
    (-1, 1, 0, 8, 16, 48),
    (-1, -1, 0, 8, 16, 49),
    (0, 0, 1, 0, 8, 22),
    (0, 2, 0, 0, 8, 10),
    (0, 1, 0, 0, 8, 20),
    (1, -2, 0, 0, 8, 11),
    (1, 0, 1, 0, 8, 23),
    (1, -1, 0, 0, 8, 21),
    (4, 1, 0, 8, 16, 18),
    (4, 0, 1, 8, 16, 2),
    (5, -1, 0, 8, 16, 19),
    (5, 0, 1, 8, 16, 3),
    (6, 0, 1, 8, 16, 8),
    (9, 1, 0, 0, 8, 14),
    (7, 0, 1, 8, 16, 9),
    (11, -1, 0, 0, 8, 15),
    (4, 4, 0, 8, 12, 36),
    (9, 0, 1, 0, 8, 31),
    (5, -4, 0, 12, 16, 37),
    (14, 1, 0, 8, 16, 33),
    (10, 0, 1, 0, 8, 16),
    (9, 3, 0, 0, 4, 42),
    (16, -1, 0, 8, 16, 34),
    (11, 0, 1, 0, 8, 32),
    (11, -3, 0, 4, 8, 43),
    (13, 0, 1, 0, 8, 17),
    (15, 2, 0, 8, 16, 26),
    (19, 1, 0, 0, 8, 0),
    (14, 0, 1, 8, 16, 24),
    (17, -2, 0, 8, 16, 27),
    (21, -1, 0, 0, 8, 1),
    (16, 0, 1, 8, 16, 25),
    (23, 1, 0, 0, 8, 12),
    (28, -1, 0, 8, 16, 39),
    (25, 1, 0, 8, 16, 38),
    (19, 1, 1, 0, 8, 6),
    (22, 0, 1, 8, 12, 44),
    (29, -1, 0, 0, 8, 13),
    (32, 1, 0, 8, 16, 28),
    (21, -1, 1, 0, 8, 7),
    (24, 0, 1, 12, 16, 45),
    (27, 0, 1, 0, 4, 46),
    (35, -1, 0, 8, 16, 29),
    (30, 0, 1, 4, 8, 47),
)
GRAD_AT = (8, 24, 46)
BACK_AT = (-1, -1, -1, -1)


def route_places():
    places = []
    for parent, dz, other, *_ in ROUTE:
        at = (0, 0) if parent < 0 else places[parent]
        places.append((at[0] - dz, at[1] ^ other))
    return places


def passed_on(parent):
    return sorted((k for k, entry in enumerate(ROUTE) if entry[0] == parent), key=lambda k: ROUTE[k][5])


def far_first(count):
    return sorted(range(count), key=lambda step: -min(step, count - step))


def layer_kernel(
    n_blk, n_rep,
    feats_hbm, cotan_hbm, weight_hbm, adj_hbm, far_hbm, ids_hbm, counts_hbm,
    out_rows, grad_feats, grad_weight,
    feats, cotan, weight, ids, counts,
    adj, far, near_x, near_p, total, pick, sent, arrived, back, returned, part, sum_rep, sum_blk, whole,
    load_sem, ring_send, ring_recv, swap_send, swap_recv, grad_send, grad_recv,
):
    blk = lax.axis_index("blk")
    rep = lax.axis_index("rep")
    rows, width = feats.shape
    groups, slots = ids.shape
    slot_total = groups * slots
    n_z = n_blk // 2
    n_y = n_rep // 4
    z = blk // 2
    x_hi = lax.rem(blk, 2)
    unit = rows // 16
    piece = part.shape[1]
    places = route_places()
    hops = sorted({(dz, other) for _, dz, other, *_ in ROUTE})

    def block_at(dz, other):
        return lax.rem(z + dz + 2 * n_z, n_z) * 2 + (1 - x_hi if other else x_hi)

    x_low, y, core = rep // (2 * n_y), lax.rem(rep // 2, n_y), lax.rem(rep, 2)
    x_parts = (x_low * (2 * n_y), (1 - x_low) * (2 * n_y))
    y_parts = [lax.rem(y + dy, n_y) * 2 for dy in range(n_y)]
    core_parts = (core, 1 - core)
    steps = [(dy, dx, dc) for dy in range(n_y) for dx in (0, 1) for dc in (0, 1) if dy or dx or dc]
    steps.sort(key=lambda step: -min(step[0], n_y - step[0]) - step[1])
    peers = [x_parts[dx] + y_parts[dy] + core_parts[dc] for dy, dx, dc in steps]
    fourth = n_rep // 4
    fourths = [peers[i:i + fourth] for i in range(0, n_rep - 1, fourth)]

    barrier = pltpu.get_barrier_semaphore()

    for hop in hops:
        pl.semaphore_signal(barrier, inc=1, device_id={"blk": block_at(*hop)}, device_id_type=MESH)

    for peer in peers:
        pl.semaphore_signal(barrier, inc=1, device_id={"rep": peer}, device_id_type=MESH)

    loads = [
        pltpu.make_async_copy(src, dst, load_sem.at[i])
        for i, (src, dst) in enumerate((
            (feats_hbm.at[0], feats), (ids_hbm.at[0, 0], ids), (counts_hbm.at[0], counts),
            (adj_hbm.at[0], adj), (far_hbm.at[0], far), (cotan_hbm.at[0], cotan), (weight_hbm, weight),
        ))
    ]
    for load in loads:
        load.start()

    def copy_on(near, phase, k):
        parent, dz, other, low, high, _ = ROUTE[k]
        at = block_at(*(places[parent] if parent >= 0 else (0, 0)))
        span = near.at[at, pl.ds(low * unit, (high - low) * unit)]
        return pltpu.make_async_remote_copy(
            src_ref=span, dst_ref=span, send_sem=ring_send.at[phase], recv_sem=ring_recv.at[phase, k],
            device_id={"blk": block_at(dz, other)}, device_id_type=MESH,
        )

    def wait_copy(near, phase, k):
        low, high = ROUTE[k][3:5]
        span = near.at[block_at(*places[k]), pl.ds(low * unit, (high - low) * unit)]
        pltpu.make_async_copy(span, span, ring_recv.at[phase, k]).wait()

    def add_pair(near, dz):
        first = lax.rem(z + dz + n_z, n_z) * 2
        columns = pl.ds(pl.multiple_of(first * rows, 2 * rows), 2 * rows)
        total[...] += dot(adj[:, columns], near[pl.ds(first, 2)].reshape(2 * rows, width))

    def ring_open(near, phase):
        for k in passed_on(-1):
            copy_on(near, phase, k).start()

    def ring_run(near, phase, between):
        seen = {0: 16}
        for task in between.get(-1, ()):
            task()
        for k in range(len(ROUTE)):
            wait_copy(near, phase, k)
            for child in passed_on(k):
                copy_on(near, phase, child).start()
            place = places[k][0] % n_z
            seen[place] = seen.get(place, 0) + ROUTE[k][4] - ROUTE[k][3]
            if seen[place] == 32:
                add_pair(near, place)
            for task in between.get(k, ()):
                task()

    def ring_drain(near, phase):
        whole_ring = near.at[pl.ds(0, n_blk - 1)]
        pltpu.make_async_copy(whole_ring, whole_ring, ring_send.at[phase]).wait()

    def to_reps(src, dst, send_sem, recv_sem, chosen):
        for peer in chosen:
            pltpu.make_async_remote_copy(
                src_ref=src(peer), dst_ref=dst, send_sem=send_sem, recv_sem=recv_sem,
                device_id={"rep": peer}, device_id_type=MESH,
            ).start()

    def wait_all(ref, count, sem):
        span = ref.at[pl.ds(0, count)]
        pltpu.make_async_copy(span, span, sem).wait()

    loads[0].wait()
    own_feats = feats[...]
    near_x[blk] = own_feats
    pl.semaphore_wait(barrier, n_rep - 1 + len(hops))
    ring_open(near_x, 0)

    def make_pick():
        spread = lax.broadcasted_iota(jnp.int32, (slots, slot_total), 1)
        within = spread - (spread // slots) * slots
        place = lax.broadcasted_iota(jnp.int32, (slots, slot_total), 0)
        per_slot = jnp.where(within == place, 1.0, 0.0).astype(BF16)
        spread_g = lax.broadcasted_iota(jnp.int32, (groups, slot_total), 1)
        own_group = (spread_g // slots) == lax.broadcasted_iota(jnp.int32, (groups, slot_total), 0)
        per_group = jnp.where(own_group, 1.0, 0.0).astype(BF16)
        loads[1].wait()
        ids_wide = dot(ids[...].astype(F32).astype(BF16), per_slot)
        ids_row = jnp.sum(jnp.where(own_group, ids_wide, 0.0), axis=0, keepdims=True)
        loads[2].wait()
        counts_low = jnp.broadcast_to(counts[...].astype(F32), (8, groups)).astype(BF16)
        counts_row = dot(counts_low, per_group)[0:1]
        live = within[0:1].astype(F32) < counts_row
        ids_row = jnp.where(live, ids_row, -1.0).astype(jnp.int32)
        row_iota = lax.broadcasted_iota(jnp.int32, (rows, slot_total), 0)
        pick[...] = jnp.where(row_iota == ids_row, 1.0, 0.0).astype(BF16)

    def gather_slots():
        sent[...] = dot(pick[...], feats[...], ((0,), (0,))).astype(BF16).reshape(groups, slots, width)
        arrived[rep] = sent[rep]

    def swap_out(chosen):
        return lambda: to_reps(lambda peer: sent.at[peer], arrived.at[rep], swap_send.at[0], swap_recv.at[0], chosen)

    def ready_adj():
        total[...] = jnp.zeros_like(total)
        loads[3].wait()

    def add_far():
        loads[4].wait()
        wait_all(arrived, n_rep - 1, swap_recv.at[0])
        total[...] += dot(far[...], arrived[...].reshape(slot_total, width))

    ring_run(near_x, 0, {-1: [make_pick, gather_slots, swap_out(peers), ready_adj], len(ROUTE) - 8: [add_far]})

    agg = total[...].astype(BF16)
    loads[5].wait()
    loads[6].wait()
    pre = dot(agg, weight[...])
    scale, cubic = 0.7978845608028654, 0.044715
    square = pre * pre
    bend = jnp.tanh(scale * pre * (1.0 + cubic * square))
    slope = 0.5 * (1.0 + bend) + 0.5 * pre * (1.0 - bend * bend) * (scale * (1.0 + 3.0 * cubic * square))
    dpre = (cotan[...].astype(F32) * slope).astype(BF16)
    proj = dot(dpre, weight[...], ((1,), (1,))).astype(BF16)
    near_p[blk] = proj
    ring_open(near_p, 1)
    share = dot(agg, dpre, ((0,), (0,)))
    per_half = n_rep // 2
    part[pl.ds(0, per_half)] = share[:, :width].reshape(per_half, piece, width)
    part[pl.ds(per_half, per_half)] = share[:, width:].reshape(per_half, piece, width)
    to_reps(lambda peer: part.at[peer], sum_rep.at[rep], grad_send.at[0], grad_recv.at[0], peers)
    sum_rep[rep] = part[rep]
    total[...] = jnp.zeros_like(total)

    def make_back():
        back[...] = dot(far[...], near_p[blk], ((0,), (0,))).astype(BF16).reshape(groups, slots, width)
        returned[rep] = back[rep]

    def swap_back(chosen):
        return lambda: to_reps(lambda peer: back.at[peer], returned.at[rep], swap_send.at[1], swap_recv.at[1], chosen)

    def grad_blk():
        wait_all(sum_rep, n_rep - 1, grad_recv.at[0])
        sum_blk[blk] = jnp.sum(sum_rep[...], axis=0)
        for dz in far_first(n_z):
            for other in (1, 0):
                if dz or other:
                    pltpu.make_async_remote_copy(
                        src_ref=sum_blk.at[blk], dst_ref=sum_blk.at[blk],
                        send_sem=grad_send.at[1], recv_sem=grad_recv.at[1],
                        device_id={"blk": block_at(dz, other)}, device_id_type=MESH,
                    ).start()

    def grad_whole():
        wait_all(sum_blk, n_blk - 1, grad_recv.at[1])
        nodes = rows * n_blk * n_rep
        whole[rep] = jnp.sum(sum_blk[...], axis=0) * (1.0 / math.sqrt(nodes))
        to_reps(lambda peer: whole.at[rep], whole.at[rep], grad_send.at[2], grad_recv.at[2], peers)

    def add_returned():
        wait_all(returned, n_rep - 1, swap_recv.at[1])
        total[...] += dot(pick[...], returned[...].reshape(slot_total, width))

    tasks = {-1: [make_back]}
    def put_rows():
        out_rows[0] = (0.5 * pre * (1.0 + bend)).astype(BF16)

    tasks[36] = [put_rows]
    for at, chosen in zip(BACK_AT, fourths):
        tasks.setdefault(at, []).append(swap_back(chosen))
    for at, task in ((GRAD_AT[0], grad_blk), (GRAD_AT[1], grad_whole), (GRAD_AT[2], add_returned)):
        tasks.setdefault(at, []).append(task)
    ring_run(near_p, 1, tasks)

    grad_feats[0] = total[...]
    wait_all(whole, n_rep - 1, grad_recv.at[2])
    flat = per_half * piece
    grad_weight[:, :width] = whole[pl.ds(0, per_half)].reshape(flat, width)
    grad_weight[:, width:] = whole[pl.ds(per_half, per_half)].reshape(flat, width)

    ring_drain(near_x, 0)
    ring_drain(near_p, 1)
    wait_all(sent, n_rep - 1, swap_send.at[0])
    wait_all(back, n_rep - 1, swap_send.at[1])
    wait_all(part, n_rep - 1, grad_send.at[0])
    wait_all(sum_blk, n_blk - 1, grad_send.at[1])
    wait_all(whole, n_rep - 1, grad_send.at[2])


def hand_out(rows_in, feats_in, weight_in, rows_out, feats_out, weight_out, rows, feats, weight, sem):
    stages = ((rows_in, rows, rows_out), (feats_in, feats, feats_out), (weight_in, weight, weight_out))
    fetches = [pltpu.make_async_copy(src, held, sem.at[0, i]) for i, (src, held, _) in enumerate(stages)]
    stores = [pltpu.make_async_copy(held, dst, sem.at[1, i]) for i, (_, held, dst) in enumerate(stages)]
    for fetch in fetches:
        fetch.start()
    for fetch, store in zip(fetches, stores):
        fetch.wait()
        store.start()
    for store in stores:
        store.wait()


def local(n_blk, n_rep, feats, cotan, weight, cycle_adj, remote_adj, send_ids, send_count):
    rows, width = feats.shape[1:]
    hidden = cotan.shape[2]
    groups, slots = send_ids.shape[2:]
    total = n_blk * rows
    piece = hidden // n_rep * (width // 128)
    vmem = pl.BlockSpec(memory_space=pltpu.VMEM)
    anywhere = pl.BlockSpec(memory_space=pl.ANY)
    dma = pltpu.SemaphoreType.DMA
    results = pl.pallas_call(
        functools.partial(layer_kernel, n_blk, n_rep),
        out_shape=(
            jax.ShapeDtypeStruct((1, rows, hidden), BF16),
            jax.ShapeDtypeStruct((1, rows, width), F32),
            jax.ShapeDtypeStruct((width, hidden), F32),
        ),
        in_specs=[anywhere] * 7,
        out_specs=(vmem, vmem, vmem),
        scratch_shapes=[
            pltpu.VMEM((rows, width), BF16),
            pltpu.VMEM((rows, hidden), BF16),
            pltpu.VMEM((width, hidden), BF16),
            pltpu.VMEM((groups, slots), jnp.int32),
            pltpu.VMEM((1, groups), jnp.int32),
            pltpu.VMEM((rows, total), BF16),
            pltpu.VMEM((rows, groups * slots), BF16),
            pltpu.VMEM((n_blk, rows, width), BF16),
            pltpu.VMEM((n_blk, rows, width), BF16),
            pltpu.VMEM((rows, width), F32),
            pltpu.VMEM((rows, groups * slots), BF16),
            pltpu.VMEM((groups, slots, width), BF16),
            pltpu.VMEM((groups, slots, width), BF16),
            pltpu.VMEM((groups, slots, width), BF16),
            pltpu.VMEM((groups, slots, width), BF16),
            pltpu.VMEM((n_rep, piece, width), F32),
            pltpu.VMEM((n_rep, piece, width), F32),
            pltpu.VMEM((n_blk, piece, width), F32),
            pltpu.VMEM((n_rep, piece, width), F32),
            dma((7,)),
            dma((2,)),
            dma((2, len(ROUTE))),
            dma((2,)),
            dma((2,)),
            dma((3,)),
            dma((3,)),
        ],
        compiler_params=pltpu.CompilerParams(
            collective_id=0, has_side_effects=True, vmem_limit_bytes=60 * 1024 * 1024
        ),
    )(feats, cotan, weight, cycle_adj, remote_adj, send_ids, send_count)
    return pl.pallas_call(
        hand_out,
        out_shape=tuple(jax.ShapeDtypeStruct(value.shape, value.dtype) for value in results),
        in_specs=[anywhere] * 3,
        out_specs=(anywhere,) * 3,
        scratch_shapes=[pltpu.VMEM(value.shape, value.dtype) for value in results] + [dma((2, 3))],
        compiler_params=pltpu.CompilerParams(vmem_limit_bytes=60 * 1024 * 1024),
    )(*results)


def solution(mesh):
    n_blk, n_rep = mesh.shape["blk"], mesh.shape["rep"]
    return jax.shard_map(
        functools.partial(local, n_blk, n_rep),
        mesh=mesh,
        in_specs=(
            P("rep", "blk", None),
            P("rep", "blk", None),
            P(),
            P("rep", "blk", None),
            P("rep", "blk", None),
            P("rep", "blk", None, None),
            P("rep", "blk", None),
        ),
        out_specs=(P("rep", "blk", None), P("rep", "blk", None), P()),
        check_vma=False,
    )
```
